256 devices in a mesh: rad: 8 (over y, x_hi), azi: 32 (over x_lo, z, core).
Axes of the slice: x: 4 (x_hi: 2, x_lo: 2; x = x_hi * 2 + x_lo), y: 4, z: 8, core: 2. Of those that a mesh axis runs over, the one named last changes fastest.
Arguments:
- density: float32 [256, 8192, 128], P('rad', 'azi'), may hold values from 0.1 to 2
- shift_cells: int32 [256], P('rad'), may hold values from 0 to 8191
- upwind_flags: int32 [256], P('rad'), may hold values 0 or 1
- courant: float32 [256, 128], P('rad'), may hold values from 0.05 to 0.9
- gain_factors: float32 [8, 128, 128], replicated, may hold values from -0.5 to 0.5
- rate_left: float32 [8, 128], replicated, may hold values from 0.1 to 1
- rate_right: float32 [8, 128], replicated, may hold values from -0.5 to 0.5
Outputs:
- evolved: float32 [256, 8192, 128], P('rad', 'azi')
The draws below stay inside these ranges and needn't reach their ends.
All inputs are finite; a program needn't handle non-finite values. No bound on the sum of `upwind_flags` on one device may be relied on, other than what follows from the above.
Results may differ from the reference program's by a relative error of at most 0.0001.
Values sent between devices are 32-bit elements; how exact they have to be, the bound alone decides.
No kernel may reach another device: no remote copies, remote signals or barrier semaphores. Data moves between devices by JAX's collectives and lax.ppermute only.
A program may use at most 64 MiB of HBM per device.

```python
import math
import jax
import jax.numpy as jnp
from jax import lax

NB = 128
RANK = 8
NR = 256
NA = 8192


def touch_ends(array, rng, low, top_value):
    longest = array.shape.index(max(array.shape))
    spots = []
    for shift in (0, 1):
        where = [jax.random.randint(jax.random.fold_in(rng, axis), (), 0, length) for axis, length in enumerate(array.shape)]
        where[longest] = (where[longest] + shift) % array.shape[longest]
        spots.append(tuple(where))
    return array.at[spots[0]].set(low).at[spots[1]].set(top_value)


def shard_levels(stream_key, dims, split, low, high):
    level = 1.0
    for position, shards_of in split:
        heights = jax.random.uniform(jax.random.fold_in(jax.random.fold_in(stream_key, 6), position), (shards_of,), jnp.float32, low / len(split), high / len(split))
        level = level * jnp.repeat(jnp.exp(heights), dims[position] // shards_of).reshape((-1,) + (1,) * (len(dims) - 1 - position))
    return level


def normal_values(key, shape, scale, bound, dtype=jnp.bfloat16):
    array = scale * jax.random.normal(key, shape, jnp.float32)
    return jnp.clip(array, min=-bound, max=bound).astype(dtype)


def setup_inputs(seed: int = 0) -> dict:
    seeds = jax.random.split(jax.random.key(seed), 8)
    return {
        "density": jnp.clip(jnp.exp(math.log(2.0) - 2.9957323 * jax.random.uniform(seeds[0], (NR, NA, NB), jnp.float32) ** shard_levels(seeds[0], (NR, NA, NB), ((0, 8), (1, 32)), -0.2, 0.2)), 0.1, 2.0),
        "shift_cells": touch_ends(jax.random.randint(seeds[1], (NR,), 0, NA), jax.random.fold_in(seeds[1], 1), 0, NA - 1).astype(jnp.int32),
        "upwind_flags": touch_ends((jax.random.randint(seeds[2], (NR,), 0, 2) < 1).astype(jnp.int32), jax.random.fold_in(seeds[2], 1), 0, 1),
        "courant": jnp.clip(jnp.exp(math.log(0.9) - 2.8903717 * jax.random.uniform(seeds[3], (NR, NB), jnp.float32) ** shard_levels(seeds[3], (NR, NB), ((0, 8),), -0.2, 0.2)), 0.05, 0.9),
        "gain_factors": normal_values(seeds[4], (RANK, NB, NB), NB ** -0.5, 0.5, jnp.float32),
        "rate_left": jnp.clip(jnp.exp(jax.random.uniform(seeds[5], (RANK, NB), jnp.float32, math.log(0.1), math.log(1.0))), 0.1, 1.0),
        "rate_right": normal_values(seeds[6], (RANK, NB), NB ** -0.5, 0.5, jnp.float32),
    }


def roll_row(row, amount):
    return jnp.roll(row, amount, axis=0)


def coagulate(block, gain_factors, rate_left, rate_right):
    cells = block.reshape(-1, block.shape[-1])
    partner = jnp.dot(cells, rate_right.T, preferred_element_type=jnp.float32, precision=lax.Precision.HIGHEST)
    loss_rate = jnp.dot(partner, rate_left, preferred_element_type=jnp.float32, precision=lax.Precision.HIGHEST)
    gain = jnp.zeros_like(cells)
    for term in range(gain_factors.shape[0]):
        mapped = jnp.dot(cells, gain_factors[term], preferred_element_type=jnp.float32, precision=lax.Precision.HIGHEST)
        gain = gain + partner[:, term:term + 1] * mapped
    result = cells + 0.25 * (gain - cells * loss_rate)
    return result.reshape(block.shape)


def reference(density, shift_cells, upwind_flags, courant, gain_factors, rate_left, rate_right):
    shifted = jax.vmap(roll_row)(density, shift_cells)
    padded = jnp.pad(shifted, ((1, 1), (0, 0), (0, 0)))
    source = jnp.where((upwind_flags == 1)[:, None, None], padded[2:], padded[:-2])
    drifted = shifted - courant[:, None, :] * (shifted - source)
    return lax.map(lambda block: coagulate(block, gain_factors, rate_left, rate_right), drifted)
```

```python
import functools

import jax
import jax.numpy as jnp
from jax import lax
from jax.experimental import pallas as pl
from jax.experimental.pallas import tpu as pltpu
from jax.sharding import PartitionSpec as P

MIB = 2**20


def roll_kernel(shift_ref, row_ref, out_ref, sem):
    cells = row_ref.shape[0]
    shift = shift_ref[0]

    @pl.when(shift > 0)
    def _():
        pltpu.make_async_copy(row_ref.at[pl.ds(cells - shift, shift)], out_ref.at[pl.ds(0, shift)], sem).start()

    pltpu.make_async_copy(row_ref.at[pl.ds(0, cells - shift)], out_ref.at[pl.ds(shift, cells - shift)], sem).start()
    pltpu.make_async_copy(row_ref, out_ref, sem).wait()


def rolled(row, shift):
    cells, bins = row.shape
    out = pl.pallas_call(
        roll_kernel,
        out_shape=jax.ShapeDtypeStruct((cells, 1, bins), row.dtype),
        in_specs=[pl.BlockSpec(memory_space=pltpu.SMEM), pl.BlockSpec(memory_space=pl.ANY)],
        out_specs=pl.BlockSpec(memory_space=pl.ANY),
        scratch_shapes=[pltpu.SemaphoreType.DMA],
        compiler_params=pltpu.CompilerParams(vmem_limit_bytes=16 * MIB),
        cost_estimate=pl.CostEstimate(flops=0, bytes_accessed=8 * cells * bins, transcendentals=0),
        name="roll",
    )(shift, row.reshape(cells, 1, bins))
    return out.reshape(cells, bins)


def split(x):
    high = x.astype(jnp.bfloat16)
    return high, (x - high.astype(jnp.float32)).astype(jnp.bfloat16)


def evolve_kernel(flags_ref, x_ref, before_ref, after_ref, courant_ref, gain_ref, left_ref, right_ref, out_ref,
                  upper_ref, lower_ref, cells_ref):
    rows, width, bins = x_ref.shape
    terms = gain_ref.shape[0]
    total = (terms + 1) * bins

    @pl.when(pl.program_id(0) == 0)
    def _():
        diagonal = lax.broadcasted_iota(jnp.int32, (bins, bins), 0) == lax.broadcasted_iota(jnp.int32, (bins, bins), 1)
        for p in range(terms):
            net = gain_ref[p] - jnp.where(diagonal, left_ref[p : p + 1, :], 0.0)
            high, low = split(0.25 * net)
            upper_ref[:bins, p * bins : (p + 1) * bins] = high
            upper_ref[bins:, p * bins : (p + 1) * bins] = high
            lower_ref[:, p * bins : (p + 1) * bins] = low
        high, low = split(right_ref[...])
        upper_ref[:bins, terms * bins : total] = high
        upper_ref[bins:, terms * bins : total] = high
        lower_ref[:, terms * bins : total] = low

    for r in range(rows):
        here = x_ref[r]
        larger = x_ref[r + 1] if r + 1 < rows else after_ref[0]
        smaller = x_ref[r - 1] if r > 0 else before_ref[0]
        source = jnp.where(flags_ref[r] == 1, larger, smaller)
        cells_ref[r * width : (r + 1) * width, :] = here - courant_ref[r : r + 1, :] * (here - source)

    chunk = min(256, rows * width)
    for start in range(0, rows * width, chunk):
        n = cells_ref[start : start + chunk, :]
        high, low = split(n)
        both = jnp.concatenate([high, low], axis=1)

        def product(first, last):
            return jnp.dot(both, upper_ref[:, first:last], preferred_element_type=jnp.float32) + jnp.dot(
                high, lower_ref[:, first:last], preferred_element_type=jnp.float32
            )

        partner = product(terms * bins, total)
        result = n
        for p in range(0, terms, 2):
            mapped = product(p * bins, (p + 2) * bins)
            result = result + partner[:, p : p + 1] * mapped[:, :bins] + partner[:, p + 1 : p + 2] * mapped[:, bins:]
        out_ref[start // width : (start + chunk) // width] = result.reshape(chunk // width, width, bins)


def evolved(shifted, before, after, upwind_flags, courant, gain_factors, rate_left, rate_right):
    rows, width, bins = shifted.shape
    terms = gain_factors.shape[0]
    step = 32
    right = jnp.zeros((bins, bins), jnp.float32).at[:, :terms].set(rate_right.T)
    whole = lambda *shape: pl.BlockSpec(shape, lambda i: (0,) * len(shape))
    return pl.pallas_call(
        evolve_kernel,
        grid=(width // step,),
        out_shape=jax.ShapeDtypeStruct(shifted.shape, shifted.dtype),
        in_specs=[
            pl.BlockSpec(memory_space=pltpu.SMEM),
            pl.BlockSpec((rows, step, bins), lambda i: (0, i, 0)),
            pl.BlockSpec((1, step, bins), lambda i: (0, i, 0)),
            pl.BlockSpec((1, step, bins), lambda i: (0, i, 0)),
            whole(rows, bins),
            whole(terms, bins, bins),
            whole(terms, bins),
            whole(bins, bins),
        ],
        out_specs=pl.BlockSpec((rows, step, bins), lambda i: (0, i, 0)),
        scratch_shapes=[
            pltpu.VMEM((2 * bins, (terms + 1) * bins), jnp.bfloat16),
            pltpu.VMEM((bins, (terms + 1) * bins), jnp.bfloat16),
            pltpu.VMEM((rows * step, bins), jnp.float32),
        ],
        compiler_params=pltpu.CompilerParams(vmem_limit_bytes=32 * MIB),
        name="evolve",
    )(upwind_flags, shifted, before, after, courant, gain_factors, rate_left, right)


def shards(density, shift_cells, upwind_flags, courant, gain_factors, rate_left, rate_right):
    rows, width, bins = density.shape
    ring, bands = lax.axis_size("azi"), lax.axis_size("rad")
    row = lax.all_to_all(density, "azi", 0, 0, tiled=True)
    shift = lax.dynamic_slice(shift_cells, (lax.axis_index("azi"),), (1,))
    row = rolled(row.reshape(ring * width, bins), shift)
    shifted = lax.all_to_all(row.reshape(ring, width, bins), "azi", 0, 0, tiled=True)
    up = [(i, i + 1) for i in range(bands - 1)]
    before = lax.ppermute(shifted[rows - 1 :], "rad", up)
    after = lax.ppermute(shifted[:1], "rad", [(j, i) for i, j in up])
    return evolved(shifted, before, after, upwind_flags, courant, gain_factors, rate_left, rate_right)


def solution(mesh):
    return jax.shard_map(
        shards,
        mesh=mesh,
        in_specs=(P("rad", "azi", None), P("rad"), P("rad"), P("rad", None), P(), P(), P()),
        out_specs=P("rad", "azi", None),
        check_vma=False,
    )
```

```python
import jax
import jax.numpy as jnp
from jax import lax
from jax.experimental import pallas as pl
from jax.experimental.pallas import tpu as pltpu
from jax.sharding import PartitionSpec as P

MIB = 2**20


def roll_kernel(shift_ref, row_ref, out_ref, held_ref, in_sems, out_sem):
    cells = row_ref.shape[0]
    parts = in_sems.shape[0]
    size = cells // parts
    shift = shift_ref[0]
    loads = [
        pltpu.make_async_copy(row_ref.at[pl.ds(k * size, size)], held_ref.at[pl.ds(k * size, size)], in_sems.at[k])
        for k in range(parts)
    ]
    for load in loads:
        load.start()
    for k in range(parts):
        loads[k].wait()
        at = lax.rem(k * size + shift, cells)
        first = jnp.minimum(size, cells - at)
        pltpu.make_async_copy(held_ref.at[pl.ds(k * size, first)], out_ref.at[pl.ds(at, first)], out_sem).start()

        @pl.when(first < size)
        def _():
            rest = size - first
            pltpu.make_async_copy(held_ref.at[pl.ds(k * size + first, rest)], out_ref.at[pl.ds(0, rest)], out_sem).start()

    pltpu.make_async_copy(held_ref, out_ref, out_sem).wait()


def rolled(row, shift):
    cells, bins = row.shape
    parts = 2
    out = pl.pallas_call(
        roll_kernel,
        out_shape=jax.ShapeDtypeStruct((cells, 1, bins), row.dtype),
        in_specs=[pl.BlockSpec(memory_space=pltpu.SMEM), pl.BlockSpec(memory_space=pl.ANY)],
        out_specs=pl.BlockSpec(memory_space=pltpu.HBM),
        scratch_shapes=[
            pltpu.VMEM((cells, 1, bins), row.dtype),
            pltpu.SemaphoreType.DMA((parts,)),
            pltpu.SemaphoreType.DMA,
        ],
        compiler_params=pltpu.CompilerParams(vmem_limit_bytes=16 * MIB),
        cost_estimate=pl.CostEstimate(flops=0, bytes_accessed=8 * cells * bins, transcendentals=0),
        name="roll",
    )(shift, row.reshape(cells, 1, bins))
    return out.reshape(cells, bins)


def split(x):
    high = x.astype(jnp.bfloat16)
    return high, (x - high.astype(jnp.float32)).astype(jnp.bfloat16)


def weights_kernel(gain_ref, left_ref, right_ref, upper_ref, lower_ref):
    terms, bins, _ = gain_ref.shape
    diagonal = lax.broadcasted_iota(jnp.int32, (bins, bins), 0) == lax.broadcasted_iota(jnp.int32, (bins, bins), 1)
    for p in range(terms):
        high, low = split(0.25 * (gain_ref[p] - jnp.where(diagonal, left_ref[p : p + 1, :], 0.0)))
        columns = slice(p * bins, (p + 1) * bins)
        upper_ref[:bins, columns] = high
        upper_ref[bins:, columns] = high
        lower_ref[:, columns] = low
    right = right_ref[...]
    right = jnp.concatenate([right, right, jnp.zeros((bins - 2 * terms, bins), jnp.float32)], axis=0).T
    high, low = split(right)
    first = lax.broadcasted_iota(jnp.int32, (bins, bins), 1) < terms
    high, low = high.astype(jnp.float32), low.astype(jnp.float32)
    upper_ref[:bins, terms * bins :] = jnp.where(first, high, low).astype(jnp.bfloat16)
    upper_ref[bins:, terms * bins :] = jnp.where(first, high, 0.0).astype(jnp.bfloat16)


def weights(gain_factors, rate_left, rate_right):
    terms, bins, _ = gain_factors.shape
    vmem = pl.BlockSpec(memory_space=pltpu.VMEM)
    return pl.pallas_call(
        weights_kernel,
        out_shape=(
            jax.ShapeDtypeStruct((2 * bins, (terms + 1) * bins), jnp.bfloat16),
            jax.ShapeDtypeStruct((bins, terms * bins), jnp.bfloat16),
        ),
        in_specs=[vmem] * 3,
        out_specs=(vmem, vmem),
        cost_estimate=pl.CostEstimate(flops=0, bytes_accessed=2 * MIB, transcendentals=0),
        name="weights",
    )(gain_factors, rate_left, rate_right)


def coagulated(n, upper_ref, lower_ref):
    bins = n.shape[1]
    terms = lower_ref.shape[1] // bins
    high, low = split(n)
    both = jnp.concatenate([high, low], axis=1)
    partner = jnp.dot(both, upper_ref[:, terms * bins :], preferred_element_type=jnp.float32)
    partner = partner + pltpu.roll(partner, bins - terms, 1)
    result = n
    for p in range(0, terms, 2):
        columns = slice(p * bins, (p + 2) * bins)
        mapped = jnp.dot(both, upper_ref[:, columns], preferred_element_type=jnp.float32) + jnp.dot(
            high, lower_ref[:, columns], preferred_element_type=jnp.float32
        )
        result = result + partner[:, p : p + 1] * mapped[:, :bins] + partner[:, p + 1 : p + 2] * mapped[:, bins:]
    return result


def drifted(here, larger, smaller, flag, courant):
    return here - courant * (here - jnp.where(flag == 1, larger, smaller))


def interior_kernel(flags_ref, x_ref, courant_ref, upper_ref, lower_ref, out_ref, cells_ref):
    rows, width, bins = x_ref.shape
    for r in range(1, rows - 1):
        cells_ref[(r - 1) * width : r * width, :] = drifted(
            x_ref[r], x_ref[r + 1], x_ref[r - 1], flags_ref[r], courant_ref[r : r + 1, :]
        )
    result = coagulated(cells_ref[...], upper_ref, lower_ref)
    out_ref[1 : rows - 1] = result.reshape(rows - 2, width, bins)


def ends_kernel(flags_ref, low_ref, high_ref, before_ref, after_ref, courant_ref, upper_ref, lower_ref, kept_ref,
                out_ref, cells_ref, sems):
    del kept_ref
    width = low_ref.shape[1]
    rows = flags_ref.shape[0]
    cells_ref[:width, :] = drifted(low_ref[0], low_ref[1], before_ref[0], flags_ref[0], courant_ref[:1, :])
    cells_ref[width:, :] = drifted(high_ref[1], after_ref[0], high_ref[0], flags_ref[rows - 1], courant_ref[rows - 1 :, :])
    cells_ref[...] = coagulated(cells_ref[...], upper_ref, lower_ref)
    copies = [
        pltpu.make_async_copy(cells_ref.at[pl.ds(k * width, width)], out_ref.at[r], sems.at[k])
        for k, r in enumerate((0, rows - 1))
    ]
    for copy in copies:
        copy.start()
    for copy in copies:
        copy.wait()


def evolved(shifted, before, after, upwind_flags, courant, upper, lower):
    rows, width, bins = shifted.shape
    step = min(64, width)
    smem, vmem = pl.BlockSpec(memory_space=pltpu.SMEM), pl.BlockSpec(memory_space=pltpu.VMEM)
    whole = lambda a: pl.BlockSpec(a.shape, lambda i: (0,) * a.ndim)
    block = pl.BlockSpec((rows, step, bins), lambda i: (0, i, 0))
    cells = (rows - 2) * width
    out = pl.pallas_call(
        interior_kernel,
        grid=(width // step,),
        out_shape=jax.ShapeDtypeStruct(shifted.shape, shifted.dtype),
        in_specs=[smem, block, whole(courant), whole(upper), whole(lower)],
        out_specs=block,
        scratch_shapes=[pltpu.VMEM(((rows - 2) * step, bins), jnp.float32)],
        compiler_params=pltpu.CompilerParams(vmem_limit_bytes=40 * MIB),
        cost_estimate=pl.CostEstimate(
            flops=2 * cells * (upper.size + lower.size), bytes_accessed=8 * shifted.size, transcendentals=0
        ),
        name="interior",
    )(upwind_flags, shifted, courant, upper, lower)
    pair = lambda at: pl.BlockSpec((2, width, bins), lambda i: (at, 0, 0))
    return pl.pallas_call(
        ends_kernel,
        grid=(1,),
        out_shape=jax.ShapeDtypeStruct(shifted.shape, shifted.dtype),
        in_specs=[
            smem, pair(0), pair(rows // 2 - 1), whole(before), whole(after), whole(courant), whole(upper), whole(lower),
            pl.BlockSpec(memory_space=pl.ANY),
        ],
        out_specs=pl.BlockSpec(memory_space=pl.ANY),
        scratch_shapes=[pltpu.VMEM((2 * width, bins), jnp.float32), pltpu.SemaphoreType.DMA((2,))],
        input_output_aliases={8: 0},
        compiler_params=pltpu.CompilerParams(vmem_limit_bytes=24 * MIB),
        name="ends",
    )(upwind_flags, shifted, shifted, before, after, courant, upper, lower, out)


def shards(density, shift_cells, upwind_flags, courant, gain_factors, rate_left, rate_right):
    rows, width, bins = density.shape
    ring, bands = lax.axis_size("azi"), lax.axis_size("rad")
    row = lax.all_to_all(density, "azi", 0, 0, tiled=True)
    shift = lax.dynamic_slice(shift_cells, (lax.axis_index("azi"),), (1,))
    row = rolled(row.reshape(ring * width, bins), shift)
    shifted = lax.all_to_all(row.reshape(ring, width, bins), "azi", 0, 0, tiled=True)
    up = [(i, i + 1) for i in range(bands - 1)]
    before = lax.ppermute(shifted[rows - 1 :], "rad", up)
    after = lax.ppermute(shifted[:1], "rad", [(j, i) for i, j in up])
    upper, lower = weights(gain_factors, rate_left, rate_right)
    return evolved(shifted, before, after, upwind_flags, courant, upper, lower)


def solution(mesh):
    return jax.shard_map(
        shards,
        mesh=mesh,
        in_specs=(P("rad", "azi", None), P("rad"), P("rad"), P("rad", None), P(), P(), P()),
        out_specs=P("rad", "azi", None),
        check_vma=False,
    )
```

```python
import jax
import jax.numpy as jnp
from jax import lax
from jax.experimental import pallas as pl
from jax.experimental.pallas import tpu as pltpu
from jax.sharding import PartitionSpec as P

MIB = 2**20


def roll_kernel(shift_ref, row_ref, out_ref, held_ref, in_sems, out_sem):
    cells = row_ref.shape[0]
    parts = in_sems.shape[0]
    size = cells // parts
    shift = shift_ref[0]
    loads = [
        pltpu.make_async_copy(row_ref.at[pl.ds(k * size, size)], held_ref.at[pl.ds(k * size, size)], in_sems.at[k])
        for k in range(parts)
    ]
    for load in loads:
        load.start()
    for k in range(parts):
        loads[k].wait()
        at = lax.rem(k * size + shift, cells)
        first = jnp.minimum(size, cells - at)
        pltpu.make_async_copy(held_ref.at[pl.ds(k * size, first)], out_ref.at[pl.ds(at, first)], out_sem).start()

        @pl.when(first < size)
        def _():
            rest = size - first
            pltpu.make_async_copy(held_ref.at[pl.ds(k * size + first, rest)], out_ref.at[pl.ds(0, rest)], out_sem).start()

    pltpu.make_async_copy(held_ref, out_ref, out_sem).wait()


def rolled(row, shift):
    cells, bins = row.shape
    parts = 4
    out = pl.pallas_call(
        roll_kernel,
        out_shape=jax.ShapeDtypeStruct((cells, 1, bins), row.dtype),
        in_specs=[pl.BlockSpec(memory_space=pltpu.SMEM), pl.BlockSpec(memory_space=pl.ANY)],
        out_specs=pl.BlockSpec(memory_space=pltpu.HBM),
        scratch_shapes=[
            pltpu.VMEM((cells, 1, bins), row.dtype),
            pltpu.SemaphoreType.DMA((parts,)),
            pltpu.SemaphoreType.DMA,
        ],
        compiler_params=pltpu.CompilerParams(vmem_limit_bytes=60 * MIB),
        cost_estimate=pl.CostEstimate(flops=0, bytes_accessed=8 * cells * bins, transcendentals=0),
        name="roll",
    )(shift, row.reshape(cells, 1, bins))
    return out.reshape(cells, bins)


def split(x):
    high = x.astype(jnp.bfloat16)
    return high, (x - high.astype(jnp.float32)).astype(jnp.bfloat16)


def weights_kernel(gain_ref, left_ref, right_ref, upper_ref, lower_ref):
    terms, bins, _ = gain_ref.shape
    diagonal = lax.broadcasted_iota(jnp.int32, (bins, bins), 0) == lax.broadcasted_iota(jnp.int32, (bins, bins), 1)
    for p in range(terms):
        high, low = split(0.25 * (gain_ref[p] - jnp.where(diagonal, left_ref[p : p + 1, :], 0.0)))
        columns = slice(p * bins, (p + 1) * bins)
        upper_ref[:bins, columns] = high
        upper_ref[bins:, columns] = high
        lower_ref[:, columns] = low
    right = right_ref[...]
    right = jnp.concatenate([right, right, jnp.zeros((bins - 2 * terms, bins), jnp.float32)], axis=0).T
    high, low = split(right)
    first = lax.broadcasted_iota(jnp.int32, (bins, bins), 1) < terms
    high, low = high.astype(jnp.float32), low.astype(jnp.float32)
    upper_ref[:bins, terms * bins :] = jnp.where(first, high, low).astype(jnp.bfloat16)
    upper_ref[bins:, terms * bins :] = jnp.where(first, high, 0.0).astype(jnp.bfloat16)


def weights(gain_factors, rate_left, rate_right):
    terms, bins, _ = gain_factors.shape
    vmem = pl.BlockSpec(memory_space=pltpu.VMEM)
    return pl.pallas_call(
        weights_kernel,
        out_shape=(
            jax.ShapeDtypeStruct((2 * bins, (terms + 1) * bins), jnp.bfloat16),
            jax.ShapeDtypeStruct((bins, terms * bins), jnp.bfloat16),
        ),
        in_specs=[vmem] * 3,
        out_specs=(vmem, vmem),
        cost_estimate=pl.CostEstimate(flops=0, bytes_accessed=2 * MIB, transcendentals=0),
        name="weights",
    )(gain_factors, rate_left, rate_right)


def coagulated(n, upper_ref, lower_ref):
    bins = n.shape[1]
    terms = lower_ref.shape[1] // bins
    high, low = split(n)
    both = jnp.concatenate([high, low], axis=1)
    partner = jnp.dot(both, upper_ref[:, terms * bins :], preferred_element_type=jnp.float32)
    partner = partner + pltpu.roll(partner, bins - terms, 1)
    result = n
    for p in range(0, terms, 2):
        columns = slice(p * bins, (p + 2) * bins)
        mapped = jnp.dot(both, upper_ref[:, columns], preferred_element_type=jnp.float32) + jnp.dot(
            high, lower_ref[:, columns], preferred_element_type=jnp.float32
        )
        result = result + partner[:, p : p + 1] * mapped[:, :bins] + partner[:, p + 1 : p + 2] * mapped[:, bins:]
    return result


def drifted(here, larger, smaller, flag, courant):
    return here - courant * (here - jnp.where(flag == 1, larger, smaller))


def interior_kernel(flags_ref, x_ref, courant_ref, upper_ref, lower_ref, out_ref, cells_ref):
    rows, width, bins = x_ref.shape
    for r in range(1, rows - 1):
        cells_ref[(r - 1) * width : r * width, :] = drifted(
            x_ref[r], x_ref[r + 1], x_ref[r - 1], flags_ref[r], courant_ref[r : r + 1, :]
        )
    result = coagulated(cells_ref[...], upper_ref, lower_ref)
    out_ref[1 : rows - 1] = result.reshape(rows - 2, width, bins)


def ends_kernel(odd_ref, flags_ref, low_ref, high_ref, first_ref, second_ref, courant_ref, upper_ref, lower_ref, kept_ref,
                out_ref, cells_ref, sems):
    del kept_ref
    width = low_ref.shape[1]
    rows = flags_ref.shape[0]
    odd = odd_ref[0] == 1
    before = jnp.where(odd, first_ref[0], second_ref[0])
    after = jnp.where(odd, second_ref[0], first_ref[0])
    cells_ref[:width, :] = drifted(low_ref[0], low_ref[1], before, flags_ref[0], courant_ref[:1, :])
    cells_ref[width:, :] = drifted(high_ref[1], after, high_ref[0], flags_ref[rows - 1], courant_ref[rows - 1 :, :])
    cells_ref[...] = coagulated(cells_ref[...], upper_ref, lower_ref)
    copies = [
        pltpu.make_async_copy(cells_ref.at[pl.ds(k * width, width)], out_ref.at[r], sems.at[k])
        for k, r in enumerate((0, rows - 1))
    ]
    for copy in copies:
        copy.start()
    for copy in copies:
        copy.wait()


def evolved(shifted, odd, first, second, upwind_flags, courant, upper, lower):
    rows, width, bins = shifted.shape
    step = min(64, width)
    smem, vmem = pl.BlockSpec(memory_space=pltpu.SMEM), pl.BlockSpec(memory_space=pltpu.VMEM)
    whole = lambda a: pl.BlockSpec(a.shape, lambda i: (0,) * a.ndim)
    block = pl.BlockSpec((rows, step, bins), lambda i: (0, i, 0))
    cells = (rows - 2) * width
    out = pl.pallas_call(
        interior_kernel,
        grid=(width // step,),
        out_shape=jax.ShapeDtypeStruct(shifted.shape, shifted.dtype),
        in_specs=[smem, block, whole(courant), whole(upper), whole(lower)],
        out_specs=block,
        scratch_shapes=[pltpu.VMEM(((rows - 2) * step, bins), jnp.float32)],
        compiler_params=pltpu.CompilerParams(vmem_limit_bytes=60 * MIB),
        cost_estimate=pl.CostEstimate(
            flops=2 * cells * (upper.size + lower.size), bytes_accessed=8 * shifted.size, transcendentals=0
        ),
        name="interior",
    )(upwind_flags, shifted, courant, upper, lower)
    pair = lambda at: pl.BlockSpec((2, width, bins), lambda i: (at, 0, 0))
    return pl.pallas_call(
        ends_kernel,
        grid=(1,),
        out_shape=jax.ShapeDtypeStruct(shifted.shape, shifted.dtype),
        in_specs=[
            smem, smem, pair(0), pair(rows // 2 - 1), whole(first), whole(second), whole(courant), whole(upper), whole(lower),
            pl.BlockSpec(memory_space=pl.ANY),
        ],
        out_specs=pl.BlockSpec(memory_space=pl.ANY),
        scratch_shapes=[pltpu.VMEM((2 * width, bins), jnp.float32), pltpu.SemaphoreType.DMA((2,))],
        input_output_aliases={9: 0},
        compiler_params=pltpu.CompilerParams(vmem_limit_bytes=24 * MIB),
        name="ends",
    )(odd, upwind_flags, shifted, shifted, first, second, courant, upper, lower, out)


def shards(density, shift_cells, upwind_flags, courant, gain_factors, rate_left, rate_right):
    rows, width, bins = density.shape
    ring, bands = lax.axis_size("azi"), lax.axis_size("rad")
    row = lax.all_to_all(density, "azi", 0, 0, tiled=True)
    shift = lax.dynamic_slice(shift_cells, (lax.axis_index("azi"),), (1,))
    row = rolled(row.reshape(ring * width, bins), shift)
    shifted = lax.all_to_all(row.reshape(ring, width, bins), "azi", 0, 0, tiled=True)
    odd = lax.rem(lax.axis_index("rad"), 2)
    top, bottom = shifted[rows - 1 :], shifted[:1]
    swaps = []
    for start, sent in ((0, jnp.where(odd == 1, bottom, top)), (1, jnp.where(odd == 1, top, bottom))):
        pairs = [(i, i + 1) for i in range(start, bands - 1, 2)]
        swaps.append(lax.ppermute(sent, "rad", pairs + [(j, i) for i, j in pairs]))
    upper, lower = weights(gain_factors, rate_left, rate_right)
    return evolved(shifted, odd[None], *swaps, upwind_flags, courant, upper, lower)


def solution(mesh):
    return jax.shard_map(
        shards,
        mesh=mesh,
        in_specs=(P("rad", "azi", None), P("rad"), P("rad"), P("rad", None), P(), P(), P()),
        out_specs=P("rad", "azi", None),
        check_vma=False,
    )
```
